256 devices in a mesh: lev: 8 (over x, core), wave: 32 (over z, y).
Axes of the slice: x: 4, y: 4, z: 8, core: 2. Of those that a mesh axis runs over, the one named last changes fastest.
Arguments:
- grid: bfloat16 [64, 4, 256, 2816], P('lev', None, 'wave'), may hold values from -6 to 6
- halo_values: float32 [32, 32, 64, 4, 128], P('wave', None, 'lev'), may hold values from -6 to 6
- halo_owner: int32 [32, 32], P('wave'), may hold values from 0 to 31, as said below
- halo_block: int32 [32, 32], P('wave'), may hold values from 0 to 175
- halo_count: int32 [32], P('wave'), may hold values from 0 to 32
- wave_list: int32 [1280], replicated, may hold values from 0 to 1279, each once
- legendre: bfloat16 [1280, 256, 1280], P(('lev', 'wave')), may hold values from -0.375 to 0.375
- modes: float32 [64, 64], replicated, may hold values from -0.75 to 0.75
- back: float32 [64, 64], replicated, may hold values from -0.75 to 0.75
- eigen: float32 [64], replicated, may hold values from 0.5 to 50
Outputs:
- spectral: bfloat16 [1280, 64, 4, 2, 1280], P(('lev', 'wave'))
The draws below stay inside these ranges and needn't reach their ends.
Inputs may be any that keep to these rules, and one draw needn't show every extreme that they name: `halo_owner`: for live slots of band w the owner differs from w by 1 to 2; at most 8 live slots of one band name one owner, and some band sends exactly 8 to each of its 4 neighbours; slots past the count hold arbitrary owners. `wave_list`: each wavenumber once.
All inputs are finite; a program needn't handle non-finite values.
Results may differ from the reference program's by a relative error of at most 0.006.
Values may be sent and summed in bfloat16 or wider, within the bound.
No kernel may reach another device: no remote copies, remote signals or barrier semaphores. Data moves between devices by JAX's collectives and lax.ppermute only.
A program may use at most 128 MiB of HBM per device.

```python
import math
import jax
import jax.numpy as jnp
from jax import lax

MW = 1280
NLON = 2816
F = 4
LEV = 64
BLK = 128
CAP = 8
REACH = 2
SLOTS = 32
NLAT = 256
NBLK = 176
N_WAVE = 32


def halo_plan(key):
    key_counts, key_full, key_other, key_order = jax.random.split(key, 4)
    band = jnp.arange(N_WAVE, dtype=jnp.int32)[:, None]
    offsets = jnp.concatenate([jnp.arange(-REACH, 0, dtype=jnp.int32), jnp.arange(1, REACH + 1, dtype=jnp.int32)])
    counts = jax.random.randint(key_counts, (N_WAVE, 2 * REACH), 0, CAP + 1)
    target = band + offsets[None, :]
    inside = (target >= 0) & (target < N_WAVE)
    counts = jnp.where(inside, counts, 0)
    full_band = jax.random.randint(key_full, (), REACH, N_WAVE - REACH)
    counts = jnp.where(band == full_band, CAP, counts).astype(jnp.int32)
    total = jnp.sum(counts, 1)
    bounds = jnp.cumsum(counts, 1)
    slot = jnp.arange(SLOTS, dtype=jnp.int32)
    which = jnp.sum((slot[None, :, None] >= bounds[:, None, :]).astype(jnp.int32), -1)
    which = jnp.minimum(which, 2 * REACH - 1)
    owner_sorted = band + offsets[which]
    other = jax.random.randint(key_other, (N_WAVE, SLOTS), 0, N_WAVE)
    live = slot[None, :] < total[:, None]
    owner_sorted = jnp.where(live, owner_sorted, other)
    score = jax.random.randint(key_order, (N_WAVE, SLOTS), 0, SLOTS)
    score = jnp.where(live, score, SLOTS + 1) * SLOTS + slot[None, :]
    order = jnp.argsort(score, axis=1, stable=True)
    owner = jnp.take_along_axis(owner_sorted, order, 1)
    return (owner.astype(jnp.int32), total.astype(jnp.int32))


def draw_halo_owner(key, part):
    owner, total = halo_plan(key)
    return owner


def draw_halo_count(key, part):
    owner, total = halo_plan(key)
    return total


def touch_ends(values, stream_key, least, high):
    place = [jax.random.randint(jax.random.fold_in(stream_key, axis), (), 0, length) for axis, length in enumerate(values.shape)]
    main_axis = values.shape.index(max(values.shape))
    beside = place[:main_axis] + [(place[main_axis] + 1) % values.shape[main_axis]] + place[main_axis + 1:]
    return values.at[tuple(place)].set(least).at[tuple(beside)].set(high)


def block_scale(key, extent, cuts, low, largest):
    def one(dim, shards_of):
        heights = jax.random.uniform(jax.random.fold_in(jax.random.fold_in(key, 6), dim), (shards_of,), jnp.float32, low / len(cuts), largest / len(cuts))
        return jnp.repeat(jnp.exp(heights), extent[dim] // shards_of).reshape((-1,) + (1,) * (len(extent) - dim - 1))

    gain = one(*cuts[0])
    for cut in cuts[1:]:
        gain = gain * one(*cut)
    return gain


def normal_values(key, shape, scale, reach, cuts=(), kind=jnp.bfloat16):
    values = jax.random.normal(key, shape, jnp.float32) * scale
    if len(cuts) > 0:
        values = block_scale(key, shape, cuts, -0.22, 0.18) * values
    return jnp.clip(values, min=-reach, max=reach).astype(kind)


def setup_inputs(seed: int = 0) -> dict:
    key_of = jax.random.split(jax.random.key(seed), 11)
    return {
        "grid": normal_values(key_of[0], (LEV, F, NLAT, NLON), 1.0, 6.0, ((0, 8), (2, 32))),
        "halo_values": normal_values(key_of[1], (N_WAVE, SLOTS, LEV, F, BLK), 1.0, 6.0, ((0, 32), (2, 8)), jnp.float32),
        "halo_owner": draw_halo_owner(jax.random.fold_in(key_of[10], 71), 0),
        "halo_block": touch_ends(jax.random.randint(key_of[3], (N_WAVE, SLOTS), 0, NBLK), jax.random.fold_in(key_of[3], 1), 0, NBLK - 1).astype(jnp.int32),
        "halo_count": draw_halo_count(jax.random.fold_in(key_of[10], 71), 0),
        "wave_list": jax.random.permutation(key_of[5], MW).astype(jnp.int32),
        "legendre": normal_values(key_of[6], (MW, NLAT, MW), NLAT ** -0.5, 0.375, ((0, 256),)),
        "modes": normal_values(key_of[7], (LEV, LEV), LEV ** -0.5, 0.75, (), jnp.float32),
        "back": normal_values(key_of[8], (LEV, LEV), LEV ** -0.5, 0.75, (), jnp.float32),
        "eigen": jnp.clip(jnp.exp(jax.random.uniform(key_of[9], (LEV,), jnp.float32, math.log(0.5), math.log(50.0))), 0.5, 50.0),
    }


def dft_table(wave_list, width):
    longitude = jnp.arange(width, dtype=jnp.int32)
    phase = longitude[:, None] * wave_list[None, :].astype(jnp.int32) % width
    angle = phase.astype(jnp.float32) * (2.0 * math.pi / width)
    scale = 1.0 / math.sqrt(width)
    return jnp.stack([jnp.cos(angle) * scale, -jnp.sin(angle) * scale], 1).astype(jnp.bfloat16)

def vertical(coefficient, modes, back, eigen, total):
    order = jnp.arange(total, dtype=jnp.float32)
    ratio = order * (order + 1.0) / (total * (total - 1.0))
    projected = jnp.einsum('skfcn,ki->sifcn', coefficient, modes, precision=lax.Precision.HIGHEST)
    scaled = projected / (1.0 + eigen[None, :, None, None, None] * ratio[None, None, None, None, :])
    return jnp.einsum('sifcn,ik->skfcn', scaled, back, precision=lax.Precision.HIGHEST)

def reference(grid, halo_values, halo_owner, halo_block, halo_count, wave_list, legendre, modes, back, eigen):
    live = (jnp.arange(SLOTS, dtype=jnp.int32)[None, :] < halo_count[:, None]).astype(jnp.float32)
    masked = halo_values * live[:, :, None, None, None]
    target = (halo_owner * NBLK + halo_block).reshape(-1).astype(jnp.int32)
    summed = jnp.zeros((N_WAVE * NBLK, LEV, F, BLK), jnp.float32).at[target].add(masked.reshape(-1, LEV, F, BLK))
    contribution = jnp.transpose(summed, (1, 2, 0, 3)).reshape(LEV, F, NLAT, NLON)
    surface = (grid.astype(jnp.float32) + contribution).astype(jnp.bfloat16)
    table = dft_table(wave_list, NLON)
    fourier = jnp.einsum('kfjx,xcs->skfcj', surface, table, preferred_element_type=jnp.float32).astype(jnp.bfloat16)
    groups = 64
    per = MW // groups
    order = jnp.arange(MW, dtype=jnp.int32)

    def one_group(items):
        piece, table_part, numbers = items
        coefficient = jnp.einsum('skfcj,sjn->skfcn', piece, table_part, preferred_element_type=jnp.float32)
        keep = (order[None, :] >= numbers[:, None]).astype(jnp.float32)
        coefficient = coefficient * keep[:, None, None, None, :]
        return vertical(coefficient, modes, back, eigen, MW).astype(jnp.bfloat16)
    result = lax.map(one_group, (fourier.reshape(groups, per, LEV, F, 2, NLAT), legendre.reshape(groups, per, NLAT, MW), wave_list.reshape(groups, per)))
    return result.reshape(MW, LEV, F, 2, MW)
```

```python
import functools
import math

import jax
import jax.numpy as jnp
import ml_dtypes
import numpy as np
from jax import lax
from jax.experimental import pallas as pl
from jax.experimental.pallas import tpu as pltpu
from jax.sharding import PartitionSpec as P

MW = 1280
NLON = 2816
F = 4
LEV = 64
BLK = 128
CAP = 8
REACH = 2
SLOTS = 32
NLAT = 256
HALF = NLON // 2
CHUNKS = NLON // BLK
OFFSETS = (-2, -1, 1, 2)
MSG = CAP * 32 + 16
BF = jnp.bfloat16
F32 = jnp.float32

MIB = 1 << 20


def half_table():
    order = np.arange(MW, dtype=np.int64).reshape(MW // 2, 2).T
    phase = order[:, :, None] * np.arange(HALF, dtype=np.int64)[None, None, :] % NLON
    angle = phase.astype(np.float32) * np.float32(2.0 * math.pi / NLON)
    scale = np.float32(1.0 / math.sqrt(NLON))
    both = np.stack([np.cos(angle) * scale, -np.sin(angle) * scale], 1)
    return both.astype(ml_dtypes.bfloat16)


def row_order():
    source = np.arange(640).reshape(4, 8, 5, 2, 2)
    target = source.transpose(2, 3, 1, 4, 0).reshape(640)
    return (target[:, None] == np.arange(640)[None, :]).astype(ml_dtypes.bfloat16)


def dot(a, b):
    return lax.dot_general(a, b, (((1,), (0,)), ((), ())), preferred_element_type=F32)


def dot_nt(a, b):
    return lax.dot_general(a, b, (((1,), (1,)), ((), ())), preferred_element_type=F32)


def pack_kernel(owner, block, count, values, *outs):
    band = lax.axis_index("wave")
    for out in outs:
        out[...] = jnp.zeros((MSG, BLK), BF)
    row = lax.broadcasted_iota(jnp.int32, (16, BLK), 0)
    place = [jnp.int32(0)] * 4
    index = [jnp.zeros((16, BLK), F32)] * 4
    for slot in range(SLOTS):
        step = owner[0, slot] - band
        live = slot < count[0]
        which = block[0, slot].astype(F32)
        for number, offset in enumerate(OFFSETS):
            hit = jnp.logical_and(live, step == offset)
            at = place[number]

            @pl.when(hit)
            def _(out=outs[number], at=at, slot=slot):
                out[pl.ds(pl.multiple_of(at * 32, 32), 32), :] = values[slot].astype(BF)

            mark = jnp.where(hit, at, -1)
            index[number] = jnp.where(row == mark, which, index[number])
            place[number] = at + hit.astype(jnp.int32)
    for out, marks in zip(outs, index):
        out[pl.ds(CAP * 32, 16), :] = marks.astype(BF)


def pack(owner, block, count, values):
    smem = pl.BlockSpec(memory_space=pltpu.SMEM)
    vmem = pl.BlockSpec(memory_space=pltpu.VMEM)
    return pl.pallas_call(
        pack_kernel,
        out_shape=[jax.ShapeDtypeStruct((MSG, BLK), BF)] * 4,
        in_specs=[smem, smem, smem, vmem],
        out_specs=[vmem] * 4,
        compiler_params=pltpu.CompilerParams(vmem_limit_bytes=8 * MIB),
        name="pack",
    )(owner, block, count, values)


def dft_kernel(
    grid, m0, m1, m2, m3, waves, table, out, acc, surf, held, four, strided, marks, marks_s, sem, sem_s
):
    copies = [
        pltpu.make_async_copy(table.at[p], held.at[p], sem.at[p]) for p in range(2)
    ]
    for copy in copies:
        copy.start()
    messages = (m0, m1, m2, m3)
    for number, message in enumerate(messages):
        marks[pl.ds(number * CAP, CAP), :] = (
            message[pl.ds(CAP * 32, 16), :].astype(F32)[:CAP].astype(jnp.int32)
        )
    to_scalar = pltpu.make_async_copy(marks, marks_s, sem_s)
    to_scalar.start()
    for kf in range(32):
        row = grid[kf].astype(F32)
        for c in range(CHUNKS):
            acc[c, pl.ds(kf, 8, stride=32), :] = row[:, c * BLK : (c + 1) * BLK]
    to_scalar.wait()
    for number, message in enumerate(messages):
        for r in range(CAP):
            b = marks_s[number * CAP + r, 0]
            j = b // CHUNKS
            c = b - j * CHUNKS
            at = pl.ds(pl.multiple_of(j * 32, 32), 32)
            acc[c, at, :] = acc[c, at, :] + message[pl.ds(r * 32, 32), :].astype(F32)
    for c in range(CHUNKS // 2):
        near, far = acc[c], acc[c + CHUNKS // 2]
        surf[0, :, c * BLK : (c + 1) * BLK] = (near + far).astype(BF)
        surf[1, :, c * BLK : (c + 1) * BLK] = (near - far).astype(BF)
    half = MW // 2
    for p in range(2):
        copies[p].wait()
        for part in range(2):
            four[p * half : (p + 1) * half, part * 256 : (part + 1) * 256] = dot_nt(
                held[p, part], surf[p]
            ).astype(BF)
    column = lax.broadcasted_iota(jnp.int32, (BLK, BLK), 1)
    for b in range(MW // BLK):
        m = waves[b : b + 1, :]
        key = (m % 2) * half + m // 2
        key = jnp.broadcast_to(key.astype(F32), (BLK, BLK)).T.astype(jnp.int32)
        pick = jnp.concatenate(
            [jnp.where(key == column + t * BLK, 1.0, 0.0).astype(BF) for t in range(MW // BLK)], 1
        )
        rows = dot(pick, four[...])
        for q in range(4):
            strided[pl.ds(q, BLK, stride=4), :] = rows[:, q * BLK : (q + 1) * BLK]
        out[b * 512 : (b + 1) * 512, :] = strided[...].astype(BF)


def dft(grid, messages, waves, table):
    vmem = pl.BlockSpec(memory_space=pltpu.VMEM)
    return pl.pallas_call(
        dft_kernel,
        out_shape=jax.ShapeDtypeStruct((MW * 4, BLK), BF),
        in_specs=[vmem] * 6 + [pl.BlockSpec(memory_space=pl.ANY)],
        out_specs=vmem,
        scratch_shapes=[
            pltpu.VMEM((CHUNKS, 256, BLK), F32),
            pltpu.VMEM((2, 256, HALF), BF),
            pltpu.VMEM((2, 2, MW // 2, HALF), BF),
            pltpu.VMEM((MW, 512), BF),
            pltpu.VMEM((512, BLK), F32),
            pltpu.VMEM((SLOTS, BLK), jnp.int32),
            pltpu.SMEM((SLOTS, BLK), jnp.int32),
            pltpu.SemaphoreType.DMA((2,)),
            pltpu.SemaphoreType.DMA,
        ],
        compiler_params=pltpu.CompilerParams(vmem_limit_bytes=32 * MIB),
        name="dft",
    )(grid, *messages, waves, table)


def prepare_kernel(modes, back, eigen, ahead, behind, scale):
    spread = jnp.where(
        lax.broadcasted_iota(jnp.int32, (256, LEV), 0) // F
        == lax.broadcasted_iota(jnp.int32, (256, LEV), 1),
        1.0,
        0.0,
    )
    picks = spread.astype(BF)
    same = (
        lax.broadcasted_iota(jnp.int32, (256, 256), 0) % F
        == lax.broadcasted_iota(jnp.int32, (256, 256), 1) % F
    )
    for source, target in ((modes, ahead), (back, behind)):
        rows = dot_nt(picks, source[...].astype(BF)).astype(BF)
        whole = dot_nt(rows, picks)
        target[...] = jnp.where(same, whole, 0.0).astype(BF)
    value = jnp.sum(spread * eigen[...], axis=1, keepdims=True)
    order = lax.broadcasted_iota(jnp.int32, (1, MW), 1).astype(F32)
    ratio = order * (order + 1.0) / (MW * (MW - 1.0))
    scale[...] = 1.0 / (1.0 + value * ratio)


def prepare(modes, back, eigen):
    vmem = pl.BlockSpec(memory_space=pltpu.VMEM)
    return pl.pallas_call(
        prepare_kernel,
        out_shape=[
            jax.ShapeDtypeStruct((256, 256), BF),
            jax.ShapeDtypeStruct((256, 256), BF),
            jax.ShapeDtypeStruct((256, MW), F32),
        ],
        in_specs=[vmem] * 3,
        out_specs=[vmem] * 3,
        compiler_params=pltpu.CompilerParams(vmem_limit_bytes=16 * MIB),
        name="prepare",
    )(modes, back, eigen)


def receive_kernel(
    waves, moved, legendre, ahead, behind, scale, order, out, sorted_rows, strided, packed, sems
):
    slot = pl.program_id(0)
    turn = lax.rem(slot, 2)

    def sends(number, turn):
        return [
            pltpu.make_async_copy(
                packed.at[turn, :, t],
                out.at[pl.ds(number * 256, 256), :, pl.ds(t * BLK, BLK)],
                sems.at[turn, t],
            )
            for t in range(MW // BLK)
        ]

    @pl.when(slot == 0)
    def _():
        for g in range(4):
            rows = [moved[lev * 640 + g * 160 : lev * 640 + (g + 1) * 160, :] for lev in range(8)]
            mixed = jnp.concatenate(
                [
                    jnp.concatenate([r[:, j * 32 : (j + 1) * 32] for r in rows], 1)
                    for j in range(4)
                ],
                0,
            )
            natural = dot(order[...], mixed).astype(BF)
            for sc in range(10):
                sorted_rows[sc, g * 64 : (g + 1) * 64, :] = natural[sc * 64 : (sc + 1) * 64]

    first = (lax.axis_index("lev") * 32 + lax.axis_index("wave")) * 5
    number = waves[first + slot]
    keep = lax.broadcasted_iota(jnp.int32, (1, MW), 1) >= number
    for part in range(2):
        projected = dot_nt(ahead[...], sorted_rows[slot * 2 + part]).astype(BF)
        scaled = dot(projected, legendre[0]) * jnp.where(keep, scale[...], 0.0)
        final = dot(behind[...], scaled.astype(BF))
        for t in range(MW // BLK):
            strided[pl.ds(t * 2 + part, 256, stride=20), :] = final[:, t * BLK : (t + 1) * BLK]

    @pl.when(slot >= 2)
    def _():
        for copy in sends(slot - 2, turn):
            copy.wait()

    packed.at[turn].reshape(5120, BLK)[...] = strided[...].astype(BF)
    for copy in sends(slot, turn):
        copy.start()

    @pl.when(slot == 4)
    def _():
        for copy in sends(slot - 1, 1 - turn) + sends(slot, turn):
            copy.wait()


def receive(waves, moved, legendre, ahead, behind, scale, order):
    vmem = pl.BlockSpec(memory_space=pltpu.VMEM)
    return pl.pallas_call(
        receive_kernel,
        grid=(5,),
        out_shape=jax.ShapeDtypeStruct((5 * 256, 2, MW), BF),
        in_specs=[
            pl.BlockSpec(memory_space=pltpu.SMEM),
            vmem,
            pl.BlockSpec((1, NLAT, MW), lambda s: (s, 0, 0)),
            vmem,
            vmem,
            vmem,
            vmem,
        ],
        out_specs=pl.BlockSpec(memory_space=pl.ANY),
        scratch_shapes=[
            pltpu.VMEM((10, 256, 256), BF),
            pltpu.VMEM((5120, BLK), F32),
            pltpu.VMEM((2, 256, MW // BLK, 2, BLK), BF),
            pltpu.SemaphoreType.DMA((2, MW // BLK)),
        ],
        compiler_params=pltpu.CompilerParams(vmem_limit_bytes=32 * MIB),
        name="receive",
    )(waves, moved, legendre, ahead, behind, scale, order)


def shards(
    table,
    order,
    grid,
    halo_values,
    halo_owner,
    halo_block,
    halo_count,
    wave_list,
    legendre,
    modes,
    back,
    eigen,
):
    bands = lax.axis_size("wave")
    sent = pack(halo_owner, halo_block, halo_count, halo_values.reshape(SLOTS, 32, BLK))
    came = []
    for message, step in zip(sent, OFFSETS):
        route = [(i, i + step) for i in range(bands) if 0 <= i + step < bands]
        came.append(lax.ppermute(message, "wave", route))
    fourier = dft(grid.reshape(32, 8, NLON), came, wave_list.reshape(10, BLK), table)
    moved = lax.all_to_all(
        fourier.reshape(256, 5, 4, BLK), ("lev", "wave"), split_axis=0, concat_axis=0, tiled=True
    ).reshape(5120, BLK)
    ahead, behind, scale = prepare(modes, back, eigen.reshape(1, LEV))
    result = receive(wave_list, moved, legendre, ahead, behind, scale, order)
    return result.reshape(5, LEV, F, 2, MW)


def solution(mesh):
    placed = (
        P("lev", None, "wave", None),
        P("wave", None, "lev", None, None),
        P("wave", None),
        P("wave", None),
        P("wave"),
        P(),
        P(("lev", "wave"), None, None),
        P(),
        P(),
        P(),
    )
    mapped = jax.shard_map(
        shards,
        mesh=mesh,
        in_specs=(P(), P()) + placed,
        out_specs=P(("lev", "wave"), None, None, None, None),
        check_vma=False,
    )
    table = half_table()
    order = row_order()

    def whole(*args):
        return mapped(jnp.asarray(table), jnp.asarray(order), *args)

    return whole
```

```python
import math

import jax
import jax.numpy as jnp
import ml_dtypes
import numpy as np
from jax import lax
from jax.experimental import pallas as pl
from jax.experimental.pallas import tpu as pltpu
from jax.sharding import PartitionSpec as P

MW = 1280
NLON = 2816
F = 4
LEV = 64
BLK = 128
CAP = 8
REACH = 2
SLOTS = 32
NLAT = 256
HALF = NLON // 2
CHUNKS = NLON // BLK
OFFSETS = (-2, -1, 1, 2)
MSG = CAP * 32 + 16
BF = jnp.bfloat16
F32 = jnp.float32

MIB = 1 << 20


def half_table():
    order = np.arange(MW, dtype=np.int64).reshape(MW // 2, 2).T
    phase = order[:, :, None] * np.arange(HALF, dtype=np.int64)[None, None, :] % NLON
    angle = phase.astype(np.float32) * np.float32(2.0 * math.pi / NLON)
    scale = np.float32(1.0 / math.sqrt(NLON))
    both = np.stack([np.cos(angle) * scale, -np.sin(angle) * scale], 1)
    return both.reshape(2, MW, HALF).astype(ml_dtypes.bfloat16)


def dot(a, b):
    return lax.dot_general(a, b, (((1,), (0,)), ((), ())), preferred_element_type=F32)


def dot_nt(a, b):
    return lax.dot_general(a, b, (((1,), (1,)), ((), ())), preferred_element_type=F32)


def pack_kernel(owner, block, count, values, *refs):
    outs = refs[:4]
    owner_s, block_s, count_s, held, lists, used, sems = refs[4:]
    copies = [
        pltpu.make_async_copy(source, target, sems.at[i])
        for i, (source, target) in enumerate(
            ((owner, owner_s), (block, block_s), (count, count_s), (values, held))
        )
    ]
    for copy in copies:
        copy.start()
    band = lax.axis_index("wave")
    for number in range(5):
        used[number] = 0
    for copy in copies[:3]:
        copy.wait()
    for slot in range(SLOTS):
        step = owner_s[0, slot] - band
        number = jnp.where(step < 0, step + REACH, step + REACH - 1)
        number = jnp.where(slot < count_s[0], jnp.clip(number, 0, 4), 4)
        at = used[number]
        lists[number, at] = slot
        used[number] = at + 1
    row = lax.broadcasted_iota(jnp.int32, (16, BLK), 0)
    copies[3].wait()
    for number, out in enumerate(outs):
        marks = jnp.zeros((16, BLK), F32)
        for at in range(CAP):
            valid = at < used[number]
            slot = jnp.where(valid, lists[number, at], 0)
            out[at * 32 : (at + 1) * 32, :] = jnp.where(valid, held[slot], 0.0).astype(BF)
            which = jnp.where(valid, block_s[0, slot], 0).astype(F32)
            marks = jnp.where(row == at, which, marks)
        out[CAP * 32 :, :] = marks.astype(BF)


def params(flops=0, read=0, room=60):
    return dict(
        compiler_params=pltpu.CompilerParams(vmem_limit_bytes=room * MIB),
        cost_estimate=pl.CostEstimate(flops=flops, bytes_accessed=read, transcendentals=0),
    )


def pack(owner, block, count, values):
    vmem = pl.BlockSpec(memory_space=pltpu.VMEM)
    return pl.pallas_call(
        pack_kernel,
        out_shape=[jax.ShapeDtypeStruct((MSG, BLK), BF)] * 4,
        in_specs=[pl.BlockSpec(memory_space=pl.ANY)] * 4,
        out_specs=[vmem] * 4,
        scratch_shapes=[
            pltpu.SMEM((1, SLOTS), jnp.int32),
            pltpu.SMEM((1, SLOTS), jnp.int32),
            pltpu.SMEM((1,), jnp.int32),
            pltpu.VMEM((SLOTS, 32, BLK), F32),
            pltpu.SMEM((5, SLOTS), jnp.int32),
            pltpu.SMEM((5,), jnp.int32),
            pltpu.SemaphoreType.DMA((4,)),
        ],
        name="pack",
        **params(read=1 << 20),
    )(owner, block, count, values)


def ready_kernel(grid, out, held, made, sems):
    parts = [
        pltpu.make_async_copy(grid.at[pl.ds(16 * i, 16)], held.at[pl.ds(16 * i, 16)], sems.at[i])
        for i in range(2)
    ]
    for part in parts:
        part.start()
    for i, part in enumerate(parts):
        part.wait()
        for c in range(CHUNKS):
            block = held[16 * i : 16 * i + 16, :, c * BLK : (c + 1) * BLK].astype(F32)
            block = jnp.swapaxes(block, 0, 1).astype(BF)
            for j in range(8):
                made[c, j * 32 + 16 * i : j * 32 + 16 * i + 16, :] = block[j]
    back = pltpu.make_async_copy(made, out, sems.at[2])
    back.start()
    back.wait()


def ready(grid):
    hbm = pl.BlockSpec(memory_space=pl.ANY)
    return pl.pallas_call(
        ready_kernel,
        out_shape=jax.ShapeDtypeStruct((CHUNKS, 256, BLK), BF),
        in_specs=[hbm],
        out_specs=hbm,
        scratch_shapes=[
            pltpu.VMEM((32, 8, NLON), BF),
            pltpu.VMEM((CHUNKS, 256, BLK), BF),
            pltpu.SemaphoreType.DMA((3,)),
        ],
        name="ready",
        **params(read=3 << 20),
    )(grid)


def dft_kernel(
    m0, m1, m2, m3, waves, rows, table, out, raw, acc, pick, surf, held, four, strided, got, marks, marks_s, sems
):
    messages = (m0, m1, m2, m3)
    from_far = [
        pltpu.make_async_copy(message, got.at[i], sems.at[i]) for i, message in enumerate(messages)
    ]
    from_grid = pltpu.make_async_copy(rows, raw, sems.at[4])
    from_table = [
        pltpu.make_async_copy(table.at[p], held.at[p], sems.at[5 + p]) for p in range(2)
    ]
    for copy in from_far + [from_grid, from_table[0]]:
        copy.start()
    for number, copy in enumerate(from_far):
        copy.wait()
        marks[pl.ds(number * CAP, CAP), :] = (
            got[number, pl.ds(CAP * 32, 16), :].astype(F32)[:CAP].astype(jnp.int32)
        )
    to_scalar = pltpu.make_async_copy(marks, marks_s, sems.at[7])
    to_scalar.start()
    from_grid.wait()
    from_table[1].start()
    acc[...] = raw[...].astype(F32)
    to_scalar.wait()
    for number in range(4):
        for r in range(CAP):
            b = marks_s[number * CAP + r, 0]
            j = b // CHUNKS
            c = b - j * CHUNKS
            at = pl.ds(pl.multiple_of(j * 32, 32), 32)
            acc[c, at, :] = acc[c, at, :] + got[number, pl.ds(r * 32, 32), :].astype(F32)
    for c in range(CHUNKS // 2):
        near, far = acc[c], acc[c + CHUNKS // 2]
        surf[0, :, c * BLK : (c + 1) * BLK] = (near + far).astype(BF)
        surf[1, :, c * BLK : (c + 1) * BLK] = (near - far).astype(BF)
    half = MW // 2
    column = lax.broadcasted_iota(jnp.int32, (BLK, BLK), 1)
    for p in range(2):
        from_table[p].wait()
        both = dot_nt(held[p], surf[p]).astype(BF)
        for b in range(p * 5, p * 5 + 5):
            m = waves[b : b + 1, :]
            key = (m % 2) * half + m // 2
            key = jnp.broadcast_to(key.astype(F32), (BLK, BLK)).T.astype(jnp.int32)
            for t in range(MW // BLK):
                pick[b * BLK : (b + 1) * BLK, t * BLK : (t + 1) * BLK] = jnp.where(
                    key == column + t * BLK, 1.0, 0.0
                ).astype(BF)
        for part in range(2):
            four[p * half : (p + 1) * half, part * 256 : (part + 1) * 256] = both[
                part * half : (part + 1) * half
            ]
    for b in range(2):
        found = dot(pick[b * half : (b + 1) * half], four[...])
        for q in range(4):
            strided[b, pl.ds(q, half, stride=4), :] = found[:, q * BLK : (q + 1) * BLK]
        out[b * 4 * half : (b + 1) * 4 * half, :] = strided[b].astype(BF)


def dft(messages, waves, rows, table):
    hbm = pl.BlockSpec(memory_space=pl.ANY)
    vmem = pl.BlockSpec(memory_space=pltpu.VMEM)
    return pl.pallas_call(
        dft_kernel,
        out_shape=jax.ShapeDtypeStruct((MW * 4, BLK), BF),
        in_specs=[hbm] * 4 + [vmem, hbm, hbm],
        out_specs=vmem,
        scratch_shapes=[
            pltpu.VMEM((CHUNKS, 256, BLK), BF),
            pltpu.VMEM((CHUNKS, 256, BLK), F32),
            pltpu.VMEM((MW, MW), BF),
            pltpu.VMEM((2, 256, HALF), BF),
            pltpu.VMEM((2, MW, HALF), BF),
            pltpu.VMEM((MW, 512), BF),
            pltpu.VMEM((2, MW * 2, BLK), F32),
            pltpu.VMEM((4, MSG, BLK), BF),
            pltpu.VMEM((SLOTS, BLK), jnp.int32),
            pltpu.SMEM((SLOTS, BLK), jnp.int32),
            pltpu.SemaphoreType.DMA((8,)),
        ],
        name="dft",
        **params(flops=4 << 30, read=16 << 20, room=60),
    )(*messages, waves, rows, table)


def prepare_kernel(modes, back, eigen, legendre, ahead, behind, scale, turned):
    row = lax.broadcasted_iota(jnp.int32, (256, 256), 0)
    place = lax.rem(row, 32) * 8 + lax.rem(row // 32, 2) * 4 + row // 64
    move = jnp.where(place == lax.broadcasted_iota(jnp.int32, (256, 256), 1), 1.0, 0.0)
    turned[0] = dot(move.astype(BF), legendre[0]).astype(BF)

    @pl.when(pl.program_id(0) == 0)
    def _():
        spread = jnp.where(
            lax.broadcasted_iota(jnp.int32, (256, LEV), 0) // F
            == lax.broadcasted_iota(jnp.int32, (256, LEV), 1),
            1.0,
            0.0,
        )
        picks = spread.astype(BF)
        row = lax.broadcasted_iota(jnp.int32, (256, 256), 0)
        column = lax.broadcasted_iota(jnp.int32, (256, 256), 1)
        same = lax.rem(row, F) == lax.rem(column, F)
        rows = dot_nt(picks, modes[...].astype(BF)).astype(BF)
        ahead[...] = jnp.where(same, dot_nt(rows, picks), 0.0).astype(BF)
        rows = dot_nt(picks, back[...].astype(BF)).astype(BF)
        single = jnp.where(same, dot_nt(rows, picks), 0.0).astype(BF)
        row = lax.broadcasted_iota(jnp.int32, (512, 256), 0)
        column = lax.broadcasted_iota(jnp.int32, (512, 256), 1)
        for part in range(2):
            chosen = jnp.where(row == column * 2 + part, 1.0, 0.0).astype(BF)
            behind[:, part * 256 : (part + 1) * 256] = dot(chosen, single).astype(BF)
        value = jnp.sum(spread * eigen[...], axis=1, keepdims=True)
        order = lax.broadcasted_iota(jnp.int32, (1, MW), 1).astype(F32)
        ratio = order * (order + 1.0) / (MW * (MW - 1.0))
        scale[...] = 1.0 / (1.0 + value * ratio)


def prepare(modes, back, eigen, legendre):
    def whole(*shape):
        return pl.BlockSpec(shape, lambda s: (0,) * len(shape))

    return pl.pallas_call(
        prepare_kernel,
        grid=(5,),
        out_shape=[
            jax.ShapeDtypeStruct((256, 256), BF),
            jax.ShapeDtypeStruct((512, 512), BF),
            jax.ShapeDtypeStruct((256, MW), F32),
            jax.ShapeDtypeStruct((5, NLAT, MW), BF),
        ],
        in_specs=[
            whole(LEV, LEV),
            whole(LEV, LEV),
            whole(1, LEV),
            pl.BlockSpec((1, NLAT, MW), lambda s: (s, 0, 0)),
        ],
        out_specs=[
            whole(256, 256),
            whole(512, 512),
            whole(256, MW),
            pl.BlockSpec((1, NLAT, MW), lambda s: (s, 0, 0)),
        ],
        name="prepare",
        **params(flops=2 << 30, read=8 << 20),
    )(modes, back, eigen, legendre)


def receive_kernel(
    waves, moved, legendre, ahead, behind, scale, out, *scratch
):
    moved_v, legendre_v, ahead_v, behind_v, scale_v, spread, latitude, projected, made, sems, sems_out = scratch
    first_copies = [
        pltpu.make_async_copy(moved.at[pl.ds(640 * lev, 640)], moved_v.at[pl.ds(640 * lev, 640)], sems.at[lev])
        for lev in range(8)
    ]
    later = [
        pltpu.make_async_copy(source, target, sems.at[8 + i])
        for i, (source, target) in enumerate(
            ((ahead, ahead_v), (scale, scale_v), (behind, behind_v))
        )
    ]
    tables = [
        pltpu.make_async_copy(legendre.at[s], legendre_v.at[s], sems.at[11 + s]) for s in range(5)
    ]
    for copy in first_copies + later + tables:
        copy.start()
    for copy in first_copies:
        copy.wait()
    for j in range(4):
        for lanes in range(2):
            mixed = jnp.concatenate(
                [
                    moved_v[lev * 640 : (lev + 1) * 640, j * 32 : (j + 1) * 32]
                    for lev in range(lanes * 4, lanes * 4 + 4)
                ],
                1,
            )
            spread[j, lanes] = mixed.astype(F32)

    def gather(s):
        for part in range(2):
            for j in range(4):
                for jq in range(2):
                    for lanes in range(2):
                        at = part * 256 + j * 64 + jq * 32
                        latitude[s, at : at + 32, lanes * BLK : (lanes + 1) * BLK] = spread[
                            j, lanes, pl.ds((2 * s + part) * 2 + jq, 32, stride=20), :
                        ].astype(BF)

    def project(s):
        projected[s] = dot_nt(ahead_v[...], latitude[s]).astype(BF)

    gather(0)
    later[0].wait()
    project(0)
    later[1].wait()
    later[2].wait()
    first = (lax.axis_index("lev") * 32 + lax.axis_index("wave")) * 5
    order = lax.broadcasted_iota(jnp.int32, (1, MW), 1)
    sends = []
    for s in range(5):
        tables[s].wait()
        if s < 4:
            gather(s + 1)
        factor = jnp.where(order >= waves[first + s], scale_v[...], 0.0)
        scaled = [
            (dot(projected[s, :, part * 256 : (part + 1) * 256], legendre_v[s]) * factor).astype(BF)
            for part in range(2)
        ]
        made.at[s].reshape(512, MW)[...] = dot(behind_v[...], jnp.concatenate(scaled, 0)).astype(BF)
        send = pltpu.make_async_copy(made.at[s], out.at[pl.ds(s * 256, 256)], sems_out.at[s])
        send.start()
        sends.append(send)
        if s < 4:
            project(s + 1)
    for send in sends:
        send.wait()


def receive(waves, moved, legendre, ahead, behind, scale):
    hbm = pl.BlockSpec(memory_space=pl.ANY)
    return pl.pallas_call(
        receive_kernel,
        out_shape=jax.ShapeDtypeStruct((5 * 256, 2, MW), BF),
        in_specs=[pl.BlockSpec(memory_space=pltpu.SMEM)] + [hbm] * 5,
        out_specs=hbm,
        scratch_shapes=[
            pltpu.VMEM((5120, BLK), BF),
            pltpu.VMEM((5, NLAT, MW), BF),
            pltpu.VMEM((256, 256), BF),
            pltpu.VMEM((512, 512), BF),
            pltpu.VMEM((256, MW), F32),
            pltpu.VMEM((4, 2, 640, BLK), F32),
            pltpu.VMEM((5, 512, 256), BF),
            pltpu.VMEM((5, 256, 512), BF),
            pltpu.VMEM((5, 256, 2, MW), BF),
            pltpu.SemaphoreType.DMA((16,)),
            pltpu.SemaphoreType.DMA((5,)),
        ],
        name="receive",
        **params(flops=6 << 30, read=14 << 20, room=60),
    )(waves, moved, legendre, ahead, behind, scale)


def shards(
    table, grid, halo_values, halo_owner, halo_block, halo_count, wave_list, legendre, modes, back, eigen
):
    bands = lax.axis_size("wave")
    sent = pack(halo_owner, halo_block, halo_count, halo_values.reshape(SLOTS, 32, BLK))
    came = []
    for message, step in zip(sent, OFFSETS):
        route = [(i, (i + step) % bands) for i in range(bands)]
        came.append(lax.ppermute(message, "wave", route))
    grid, _ = lax.optimization_barrier((grid, sent))
    rows = ready(grid.reshape(32, 8, NLON))
    fourier = dft(came, wave_list.reshape(10, BLK), rows, table)
    moved = lax.all_to_all(
        fourier.reshape(256, 5, 4, BLK), ("lev", "wave"), split_axis=0, concat_axis=0, tiled=True
    ).reshape(5120, BLK)
    legendre, _ = lax.optimization_barrier((legendre, fourier))
    ahead, behind, scale, turned = prepare(modes, back, eigen.reshape(1, LEV), legendre)
    result = receive(wave_list, moved, turned, ahead, behind, scale)
    return result.reshape(5, LEV, F, 2, MW)


def solution(mesh):
    placed = (
        P("lev", None, "wave", None),
        P("wave", None, "lev", None, None),
        P("wave", None),
        P("wave", None),
        P("wave"),
        P(),
        P(("lev", "wave"), None, None),
        P(),
        P(),
        P(),
    )
    mapped = jax.shard_map(
        shards,
        mesh=mesh,
        in_specs=(P(),) + placed,
        out_specs=P(("lev", "wave"), None, None, None, None),
        check_vma=False,
    )
    table = half_table()

    def whole(*args):
        return mapped(jnp.asarray(table), *args)

    return whole
```

```python
import math

import jax
import jax.numpy as jnp
import ml_dtypes
import numpy as np
from jax import lax
from jax.experimental import pallas as pl
from jax.experimental.pallas import tpu as pltpu
from jax.sharding import PartitionSpec as P

MW = 1280
NLON = 2816
F = 4
LEV = 64
BLK = 128
CAP = 8
REACH = 2
SLOTS = 32
NLAT = 256
HALF = NLON // 2
CHUNKS = NLON // BLK
OFFSETS = (-2, -1, 1, 2)
MSG = CAP * 32 + 16
BF = jnp.bfloat16
F32 = jnp.float32

MIB = 1 << 20


def half_table():
    order = np.arange(MW, dtype=np.int64).reshape(MW // 2, 2).T
    phase = order[:, :, None] * np.arange(HALF, dtype=np.int64)[None, None, :] % NLON
    angle = phase.astype(np.float32) * np.float32(2.0 * math.pi / NLON)
    scale = np.float32(1.0 / math.sqrt(NLON))
    both = np.stack([np.cos(angle) * scale, -np.sin(angle) * scale], 1)
    return both.reshape(2, MW, HALF).astype(ml_dtypes.bfloat16)


def dot(a, b):
    return lax.dot_general(a, b, (((1,), (0,)), ((), ())), preferred_element_type=F32)


def dot_nt(a, b):
    return lax.dot_general(a, b, (((1,), (1,)), ((), ())), preferred_element_type=F32)


def pack_kernel(owner, block, count, values, *refs):
    outs = refs[:4]
    owner_s, block_s, count_s, held, lists, used, sems = refs[4:]
    copies = [
        pltpu.make_async_copy(source, target, sems.at[i])
        for i, (source, target) in enumerate(
            ((owner, owner_s), (block, block_s), (count, count_s), (values, held))
        )
    ]
    for copy in copies:
        copy.start()
    band = lax.axis_index("wave")
    for number in range(5):
        used[number] = 0
    for copy in copies[:3]:
        copy.wait()
    for slot in range(SLOTS):
        step = owner_s[0, slot] - band
        number = jnp.where(step < 0, step + REACH, step + REACH - 1)
        number = jnp.where(slot < count_s[0], jnp.clip(number, 0, 4), 4)
        at = used[number]
        lists[number, at] = slot
        used[number] = at + 1
    row = lax.broadcasted_iota(jnp.int32, (16, BLK), 0)
    copies[3].wait()
    for number, out in enumerate(outs):
        marks = jnp.zeros((16, BLK), F32)
        for at in range(CAP):
            valid = at < used[number]
            slot = jnp.where(valid, lists[number, at], 0)
            out[at * 32 : (at + 1) * 32, :] = jnp.where(valid, held[slot], 0.0).astype(BF)
            which = jnp.where(valid, block_s[0, slot], 0).astype(F32)
            marks = jnp.where(row == at, which, marks)
        out[CAP * 32 :, :] = marks.astype(BF)


def params(room, flops=0, read=0):
    return dict(
        compiler_params=pltpu.CompilerParams(vmem_limit_bytes=int(room * MIB)),
        cost_estimate=pl.CostEstimate(flops=flops, bytes_accessed=read, transcendentals=0),
    )


def pack(owner, block, count, values):
    vmem = pl.BlockSpec(memory_space=pltpu.VMEM)
    return pl.pallas_call(
        pack_kernel,
        out_shape=[jax.ShapeDtypeStruct((MSG, BLK), BF)] * 4,
        in_specs=[pl.BlockSpec(memory_space=pl.ANY)] * 4,
        out_specs=[vmem] * 4,
        scratch_shapes=[
            pltpu.SMEM((1, SLOTS), jnp.int32),
            pltpu.SMEM((1, SLOTS), jnp.int32),
            pltpu.SMEM((1,), jnp.int32),
            pltpu.VMEM((SLOTS, 32, BLK), F32),
            pltpu.SMEM((5, SLOTS), jnp.int32),
            pltpu.SMEM((5,), jnp.int32),
            pltpu.SemaphoreType.DMA((4,)),
        ],
        name="pack",
        **params(60, read=1 << 20),
    )(owner, block, count, values)


def ready_kernel(grid, table, made, table_v, held, sems):
    whole = pltpu.make_async_copy(table, table_v, sems.at[2])
    parts = [
        pltpu.make_async_copy(grid.at[pl.ds(16 * i, 16)], held.at[pl.ds(16 * i, 16)], sems.at[i])
        for i in range(2)
    ]
    for part in parts + [whole]:
        part.start()
    for i, part in enumerate(parts):
        part.wait()
        for c in range(CHUNKS):
            block = held[16 * i : 16 * i + 16, :, c * BLK : (c + 1) * BLK].astype(F32)
            block = jnp.swapaxes(block, 0, 1).astype(BF)
            for j in range(8):
                made[c, j * 32 + 16 * i : j * 32 + 16 * i + 16, :] = block[j]
    whole.wait()


def ready(grid, table):
    hbm = pl.BlockSpec(memory_space=pltpu.HBM)
    vmem = pl.BlockSpec(memory_space=pltpu.VMEM)
    return pl.pallas_call(
        ready_kernel,
        out_shape=[
            jax.ShapeDtypeStruct((CHUNKS, 256, BLK), BF),
            jax.ShapeDtypeStruct(table.shape, BF),
        ],
        in_specs=[hbm, hbm],
        out_specs=[vmem, vmem],
        scratch_shapes=[
            pltpu.VMEM((32, 8, NLON), BF),
            pltpu.SemaphoreType.DMA((3,)),
        ],
        name="ready",
        **params(46, read=10 << 20),
    )(grid, table)


def dft_kernel(
    m0, m1, m2, m3, waves, raw, even, odd, out, acc, pick, surf, four, strided, marks, marks_s, sem
):
    messages = (m0, m1, m2, m3)
    for number, message in enumerate(messages):
        marks[pl.ds(number * CAP, CAP), :] = (
            message[pl.ds(CAP * 32, 16), :].astype(F32)[:CAP].astype(jnp.int32)
        )
    to_scalar = pltpu.make_async_copy(marks, marks_s, sem)
    to_scalar.start()
    acc[...] = raw[...].astype(F32)
    to_scalar.wait()
    for number, message in enumerate(messages):
        for r in range(CAP):
            b = marks_s[number * CAP + r, 0]
            j = b // CHUNKS
            c = b - j * CHUNKS
            at = pl.ds(pl.multiple_of(j * 32, 32), 32)
            acc[c, at, :] = acc[c, at, :] + message[pl.ds(r * 32, 32), :].astype(F32)
    for c in range(CHUNKS // 2):
        near, far = acc[c], acc[c + CHUNKS // 2]
        surf[0, :, c * BLK : (c + 1) * BLK] = (near + far).astype(BF)
        surf[1, :, c * BLK : (c + 1) * BLK] = (near - far).astype(BF)
    half = MW // 2
    column = lax.broadcasted_iota(jnp.int32, (BLK, BLK), 1)
    for p, table in enumerate((even, odd)):
        both = dot_nt(table[...], surf[p]).astype(BF)
        for b in range(p * 5, p * 5 + 5):
            m = waves[b : b + 1, :]
            key = (m % 2) * half + m // 2
            key = jnp.broadcast_to(key.astype(F32), (BLK, BLK)).T.astype(jnp.int32)
            for t in range(MW // BLK):
                pick[b * BLK : (b + 1) * BLK, t * BLK : (t + 1) * BLK] = jnp.where(
                    key == column + t * BLK, 1.0, 0.0
                ).astype(BF)
        for part in range(2):
            four[p * half : (p + 1) * half, part * 256 : (part + 1) * 256] = both[
                part * half : (part + 1) * half
            ]
    for b in range(2):
        found = dot(pick[b * half : (b + 1) * half], four[...])
        for q in range(4):
            strided[b, pl.ds(q, half, stride=4), :] = found[:, q * BLK : (q + 1) * BLK]
        out[b * 4 * half : (b + 1) * 4 * half, :] = strided[b].astype(BF)


def dft(messages, waves, rows, even, odd):
    vmem = pl.BlockSpec(memory_space=pltpu.VMEM)
    return pl.pallas_call(
        dft_kernel,
        out_shape=jax.ShapeDtypeStruct((MW * 4, BLK), BF),
        in_specs=[vmem] * 8,
        out_specs=vmem,
        scratch_shapes=[
            pltpu.VMEM((CHUNKS, 256, BLK), F32),
            pltpu.VMEM((MW, MW), BF),
            pltpu.VMEM((2, 256, HALF), BF),
            pltpu.VMEM((MW, 512), BF),
            pltpu.VMEM((2, MW * 2, BLK), F32),
            pltpu.VMEM((SLOTS, BLK), jnp.int32),
            pltpu.SMEM((SLOTS, BLK), jnp.int32),
            pltpu.SemaphoreType.DMA,
        ],
        name="dft",
        **params(44, flops=4 << 30, read=16 << 20),
    )(*messages, waves, rows, even, odd)


def prepare_kernel(modes, back, eigen, legendre, ahead, behind, scale, turned, held, sems):
    copies = [pltpu.make_async_copy(legendre.at[s], held.at[s], sems.at[s]) for s in range(5)]
    for copy in copies:
        copy.start()
    row = lax.broadcasted_iota(jnp.int32, (256, 256), 0)
    place = lax.rem(row, 32) * 8 + lax.rem(row // 32, 2) * 4 + row // 64
    move = jnp.where(place == lax.broadcasted_iota(jnp.int32, (256, 256), 1), 1.0, 0.0)
    spread = jnp.where(
        lax.broadcasted_iota(jnp.int32, (256, LEV), 0) // F
        == lax.broadcasted_iota(jnp.int32, (256, LEV), 1),
        1.0,
        0.0,
    )
    picks = spread.astype(BF)
    row = lax.broadcasted_iota(jnp.int32, (256, 256), 0)
    column = lax.broadcasted_iota(jnp.int32, (256, 256), 1)
    same = lax.rem(row, F) == lax.rem(column, F)
    rows = dot_nt(picks, modes[...].astype(BF)).astype(BF)
    ahead[...] = jnp.where(same, dot_nt(rows, picks), 0.0).astype(BF)
    rows = dot_nt(picks, back[...].astype(BF)).astype(BF)
    single = jnp.where(same, dot_nt(rows, picks), 0.0).astype(BF)
    row = lax.broadcasted_iota(jnp.int32, (512, 256), 0)
    column = lax.broadcasted_iota(jnp.int32, (512, 256), 1)
    for part in range(2):
        chosen = jnp.where(row == column * 2 + part, 1.0, 0.0).astype(BF)
        behind[:, part * 256 : (part + 1) * 256] = dot(chosen, single).astype(BF)
    value = jnp.sum(spread * eigen[...], axis=1, keepdims=True)
    order = lax.broadcasted_iota(jnp.int32, (1, MW), 1).astype(F32)
    ratio = order * (order + 1.0) / (MW * (MW - 1.0))
    scale[...] = 1.0 / (1.0 + value * ratio)
    for s, copy in enumerate(copies):
        copy.wait()
        turned[s] = dot(move.astype(BF), held[s]).astype(BF)


def prepare(modes, back, eigen, legendre):
    vmem = pl.BlockSpec(memory_space=pltpu.VMEM)
    return pl.pallas_call(
        prepare_kernel,
        out_shape=[
            jax.ShapeDtypeStruct((256, 256), BF),
            jax.ShapeDtypeStruct((512, 512), BF),
            jax.ShapeDtypeStruct((256, MW), F32),
            jax.ShapeDtypeStruct((5, NLAT, MW), BF),
        ],
        in_specs=[vmem] * 3 + [pl.BlockSpec(memory_space=pltpu.HBM)],
        out_specs=[vmem] * 4,
        scratch_shapes=[pltpu.VMEM((5, NLAT, MW), BF), pltpu.SemaphoreType.DMA((5,))],
        name="prepare",
        **params(16, flops=2 << 30, read=8 << 20),
    )(modes, back, eigen, legendre)


def receive_kernel(
    waves, moved, legendre, ahead, behind, scale, out, spread, latitude, projected, made, tables, sems, sems_out
):
    copies = [pltpu.make_async_copy(legendre.at[s], tables.at[s], sems.at[s]) for s in range(5)]
    for copy in copies:
        copy.start()
    for j in range(4):
        for lanes in range(2):
            mixed = jnp.concatenate(
                [
                    moved[lev * 640 : (lev + 1) * 640, j * 32 : (j + 1) * 32]
                    for lev in range(lanes * 4, lanes * 4 + 4)
                ],
                1,
            )
            spread[j, lanes] = mixed.astype(F32)

    def gather(s):
        for part in range(2):
            for j in range(4):
                for jq in range(2):
                    for lanes in range(2):
                        at = part * 256 + j * 64 + jq * 32
                        latitude[s, at : at + 32, lanes * BLK : (lanes + 1) * BLK] = spread[
                            j, lanes, pl.ds((2 * s + part) * 2 + jq, 32, stride=20), :
                        ].astype(BF)

    def project(s):
        projected[s] = dot_nt(ahead[...], latitude[s]).astype(BF)

    gather(0)
    project(0)
    first = (lax.axis_index("lev") * 32 + lax.axis_index("wave")) * 5
    order = lax.broadcasted_iota(jnp.int32, (1, MW), 1)
    sends = []
    for s in range(5):
        copies[s].wait()
        if s < 4:
            gather(s + 1)
        factor = jnp.where(order >= waves[first + s], scale[...], 0.0)
        scaled = [
            (dot(projected[s, :, part * 256 : (part + 1) * 256], tables[s]) * factor).astype(BF)
            for part in range(2)
        ]
        made.at[s].reshape(512, MW)[...] = dot(behind[...], jnp.concatenate(scaled, 0)).astype(BF)
        send = pltpu.make_async_copy(made.at[s], out.at[pl.ds(s * 256, 256)], sems_out.at[s])
        send.start()
        sends.append(send)
        if s < 4:
            project(s + 1)
    for send in sends:
        send.wait()


def receive(waves, moved, legendre, ahead, behind, scale):
    hbm = pl.BlockSpec(memory_space=pl.ANY)
    return pl.pallas_call(
        receive_kernel,
        out_shape=jax.ShapeDtypeStruct((5 * 256, 2, MW), BF),
        in_specs=[pl.BlockSpec(memory_space=pltpu.SMEM)]
        + [pl.BlockSpec(memory_space=pltpu.VMEM)]
        + [hbm]
        + [pl.BlockSpec(memory_space=pltpu.VMEM)] * 3,
        out_specs=hbm,
        scratch_shapes=[
            pltpu.VMEM((4, 2, 640, BLK), F32),
            pltpu.VMEM((5, 512, 256), BF),
            pltpu.VMEM((5, 256, 512), BF),
            pltpu.VMEM((5, 256, 2, MW), BF),
            pltpu.VMEM((5, NLAT, MW), BF),
            pltpu.SemaphoreType.DMA((5,)),
            pltpu.SemaphoreType.DMA((5,)),
        ],
        name="receive",
        **params(48, flops=6 << 30, read=14 << 20),
    )(waves, moved, legendre, ahead, behind, scale)


def shards(
    even, odd, grid, halo_values, halo_owner, halo_block, halo_count, wave_list, legendre, modes, back, eigen
):
    bands = lax.axis_size("wave")
    sent = pack(halo_owner, halo_block, halo_count, halo_values.reshape(SLOTS, 32, BLK))
    came = []
    for message, step in zip(sent, OFFSETS):
        route = [(i, (i + step) % bands) for i in range(bands)]
        came.append(lax.ppermute(message, "wave", route))
    grid, _ = lax.optimization_barrier((grid, sent))
    rows, even = ready(grid.reshape(32, 8, NLON), even)
    fourier = dft(came, wave_list.reshape(10, BLK), rows, even, odd)
    moved = lax.all_to_all(
        fourier.reshape(256, 5, 4, BLK), ("lev", "wave"), split_axis=0, concat_axis=0, tiled=True
    ).reshape(5120, BLK)
    legendre, _ = lax.optimization_barrier((legendre, fourier))
    ahead, behind, scale, turned = prepare(modes, back, eigen.reshape(1, LEV), legendre)
    result = receive(wave_list, moved, turned, ahead, behind, scale)
    return result.reshape(5, LEV, F, 2, MW)


def solution(mesh):
    placed = (
        P("lev", None, "wave", None),
        P("wave", None, "lev", None, None),
        P("wave", None),
        P("wave", None),
        P("wave"),
        P(),
        P(("lev", "wave"), None, None),
        P(),
        P(),
        P(),
    )
    mapped = jax.shard_map(
        shards,
        mesh=mesh,
        in_specs=(P(), P()) + placed,
        out_specs=P(("lev", "wave"), None, None, None, None),
        check_vma=False,
    )
    table = half_table()

    def whole(*args):
        return mapped(jnp.asarray(table[0]), jnp.asarray(table[1]), *args)

    return whole
```

```python
import math

import jax
import jax.numpy as jnp
import ml_dtypes
import numpy as np
from jax import lax
from jax.experimental import pallas as pl
from jax.experimental.pallas import tpu as pltpu
from jax.sharding import PartitionSpec as P

MW = 1280
NLON = 2816
F = 4
LEV = 64
BLK = 128
CAP = 8
SENDS = 4
REACH = 2
SLOTS = 32
NLAT = 256
HALF = NLON // 2
CHUNKS = NLON // BLK
OFFSETS = (-2, -1, 1, 2)
MSG = CAP * 32 + 16
BF = jnp.bfloat16
F32 = jnp.float32

MIB = 1 << 20


def half_table():
    order = np.arange(MW, dtype=np.int64).reshape(MW // 2, 2).T
    phase = order[:, :, None] * np.arange(HALF, dtype=np.int64)[None, None, :] % NLON
    angle = phase.astype(np.float32) * np.float32(2.0 * math.pi / NLON)
    scale = np.float32(1.0 / math.sqrt(NLON))
    both = np.stack([np.cos(angle) * scale, -np.sin(angle) * scale], 1)
    return both.reshape(2, MW, HALF).astype(ml_dtypes.bfloat16)


def dot(a, b):
    return lax.dot_general(a, b, (((1,), (0,)), ((), ())), preferred_element_type=F32)


def dot_nt(a, b):
    return lax.dot_general(a, b, (((1,), (1,)), ((), ())), preferred_element_type=F32)


def pack_kernel(owner, block, count, values, *refs):
    outs = refs[:4]
    owner_s, block_s, count_s, held, lists, used, sems = refs[4:]
    copies = [
        pltpu.make_async_copy(source, target, sems.at[i])
        for i, (source, target) in enumerate(
            ((owner, owner_s), (block, block_s), (count, count_s), (values, held))
        )
    ]
    for copy in copies:
        copy.start()
    band = lax.axis_index("wave")
    for number in range(5):
        used[number] = 0
    for copy in copies[:3]:
        copy.wait()
    for slot in range(SLOTS):
        step = owner_s[0, slot] - band
        number = jnp.where(step < 0, step + REACH, step + REACH - 1)
        number = jnp.where(slot < count_s[0], jnp.clip(number, 0, 4), 4)
        at = used[number]
        lists[number, at] = slot
        used[number] = at + 1
    row = lax.broadcasted_iota(jnp.int32, (16, BLK), 0)
    copies[3].wait()
    for number, out in enumerate(outs):
        marks = jnp.zeros((16, BLK), F32)
        for at in range(CAP):
            valid = at < used[number]
            slot = jnp.where(valid, lists[number, at], 0)
            out[at * 32 : (at + 1) * 32, :] = jnp.where(valid, held[slot], 0.0).astype(BF)
            which = jnp.where(valid, block_s[0, slot], 0).astype(F32)
            marks = jnp.where(row == at, which, marks)
        out[CAP * 32 :, :] = marks.astype(BF)


def params(room, flops=0, read=0):
    return dict(
        compiler_params=pltpu.CompilerParams(vmem_limit_bytes=int(room * MIB)),
        cost_estimate=pl.CostEstimate(flops=flops, bytes_accessed=read, transcendentals=0),
    )


def pack(owner, block, count, values):
    vmem = pl.BlockSpec(memory_space=pltpu.VMEM)
    return pl.pallas_call(
        pack_kernel,
        out_shape=[jax.ShapeDtypeStruct((MSG, BLK), BF)] * 4,
        in_specs=[pl.BlockSpec(memory_space=pl.ANY)] * 4,
        out_specs=[vmem] * 4,
        scratch_shapes=[
            pltpu.SMEM((1, SLOTS), jnp.int32),
            pltpu.SMEM((1, SLOTS), jnp.int32),
            pltpu.SMEM((1,), jnp.int32),
            pltpu.VMEM((SLOTS, 32, BLK), F32),
            pltpu.SMEM((5, SLOTS), jnp.int32),
            pltpu.SMEM((5,), jnp.int32),
            pltpu.SemaphoreType.DMA((4,)),
        ],
        name="pack",
        **params(60, read=1 << 20),
    )(owner, block, count, values)


def ready_kernel(grid, table, made, table_v, sem):
    whole = pltpu.make_async_copy(table, table_v, sem)
    whole.start()
    for i in range(2):
        for c in range(CHUNKS):
            block = grid[16 * i : 16 * i + 16, :, c * BLK : (c + 1) * BLK].astype(F32)
            block = jnp.swapaxes(block, 0, 1).astype(BF)
            for j in range(8):
                made[c, j * 32 + 16 * i : j * 32 + 16 * i + 16, :] = block[j]
    whole.wait()


def ready(grid, table):
    hbm = pl.BlockSpec(memory_space=pltpu.HBM)
    vmem = pl.BlockSpec(memory_space=pltpu.VMEM)
    return pl.pallas_call(
        ready_kernel,
        out_shape=[
            jax.ShapeDtypeStruct((CHUNKS, 256, BLK), BF),
            jax.ShapeDtypeStruct(table.shape, BF),
        ],
        in_specs=[vmem, hbm],
        out_specs=[vmem, vmem],
        scratch_shapes=[pltpu.SemaphoreType.DMA],
        name="ready",
        **params(46, read=10 << 20),
    )(grid, table)


def dft_kernel(
    m0, m1, m2, m3, waves, raw, even, odd, out, acc, pick, surf, four, strided, leaving, marks, marks_s, sem, sems
):
    messages = (m0, m1, m2, m3)
    for number, message in enumerate(messages):
        marks[pl.ds(number * CAP, CAP), :] = (
            message[pl.ds(CAP * 32, 16), :].astype(F32)[:CAP].astype(jnp.int32)
        )
    to_scalar = pltpu.make_async_copy(marks, marks_s, sem)
    to_scalar.start()
    acc[...] = raw[...].astype(F32)
    to_scalar.wait()
    for number, message in enumerate(messages):
        for r in range(CAP):
            b = marks_s[number * CAP + r, 0]
            j = b // CHUNKS
            c = b - j * CHUNKS
            at = pl.ds(pl.multiple_of(j * 32, 32), 32)
            acc[c, at, :] = acc[c, at, :] + message[pl.ds(r * 32, 32), :].astype(F32)
    for c in range(CHUNKS // 2):
        near, far = acc[c], acc[c + CHUNKS // 2]
        surf[0, :, c * BLK : (c + 1) * BLK] = (near + far).astype(BF)
        surf[1, :, c * BLK : (c + 1) * BLK] = (near - far).astype(BF)
    half = MW // 2
    column = lax.broadcasted_iota(jnp.int32, (BLK, BLK), 1)
    for p, table in enumerate((even, odd)):
        for b in range(p * 5, p * 5 + 5):
            m = waves[b : b + 1, :]
            key = (m % 2) * half + m // 2
            key = jnp.broadcast_to(key.astype(F32), (BLK, BLK)).T.astype(jnp.int32)
            for t in range(MW // BLK):
                pick[b * BLK : (b + 1) * BLK, t * BLK : (t + 1) * BLK] = jnp.where(
                    key == column + t * BLK, 1.0, 0.0
                ).astype(BF)
        both = dot_nt(table[...], surf[p]).astype(BF)
        for part in range(2):
            four[p * half : (p + 1) * half, part * 256 : (part + 1) * 256] = both[
                part * half : (part + 1) * half
            ]
    slots = MW // SENDS
    sends = []
    for b in range(SENDS):
        found = dot(pick[b * slots : (b + 1) * slots], four[...])
        for q in range(4):
            strided[b, pl.ds(q, slots, stride=4), :] = found[:, q * BLK : (q + 1) * BLK]
        rows = pl.ds(b * 4 * slots, 4 * slots)
        leaving[rows, :] = strided[b].astype(BF)
        send = pltpu.make_async_copy(leaving.at[rows], out.at[rows], sems.at[b])
        send.start()
        sends.append(send)
    for send in sends:
        send.wait()


def dft(messages, waves, rows, even, odd):
    vmem = pl.BlockSpec(memory_space=pltpu.VMEM)
    return pl.pallas_call(
        dft_kernel,
        out_shape=jax.ShapeDtypeStruct((MW * 4, BLK), BF),
        in_specs=[vmem] * 8,
        out_specs=pl.BlockSpec(memory_space=pl.ANY),
        scratch_shapes=[
            pltpu.VMEM((CHUNKS, 256, BLK), F32),
            pltpu.VMEM((MW, MW), BF),
            pltpu.VMEM((2, 256, HALF), BF),
            pltpu.VMEM((MW, 512), BF),
            pltpu.VMEM((SENDS, MW * 4 // SENDS, BLK), F32),
            pltpu.VMEM((MW * 4, BLK), BF),
            pltpu.VMEM((SLOTS, BLK), jnp.int32),
            pltpu.SMEM((SLOTS, BLK), jnp.int32),
            pltpu.SemaphoreType.DMA,
            pltpu.SemaphoreType.DMA((SENDS,)),
        ],
        name="dft",
        **params(44, flops=4 << 30, read=16 << 20),
    )(*messages, waves, rows, even, odd)


def prepare_kernel(modes, back, eigen, legendre, ahead, behind, scale, turned, held, sems):
    copies = [pltpu.make_async_copy(legendre.at[s], held.at[s], sems.at[s]) for s in range(5)]
    for copy in copies:
        copy.start()
    row = lax.broadcasted_iota(jnp.int32, (256, 256), 0)
    place = lax.rem(row, 32) * 8 + lax.rem(row // 32, 2) * 4 + row // 64
    move = jnp.where(place == lax.broadcasted_iota(jnp.int32, (256, 256), 1), 1.0, 0.0)
    spread = jnp.where(
        lax.broadcasted_iota(jnp.int32, (256, LEV), 0) // F
        == lax.broadcasted_iota(jnp.int32, (256, LEV), 1),
        1.0,
        0.0,
    )
    picks = spread.astype(BF)
    row = lax.broadcasted_iota(jnp.int32, (256, 256), 0)
    column = lax.broadcasted_iota(jnp.int32, (256, 256), 1)
    same = lax.rem(row, F) == lax.rem(column, F)
    rows = dot_nt(picks, modes[...].astype(BF)).astype(BF)
    ahead[...] = jnp.where(same, dot_nt(rows, picks), 0.0).astype(BF)
    rows = dot_nt(picks, back[...].astype(BF)).astype(BF)
    single = jnp.where(same, dot_nt(rows, picks), 0.0).astype(BF)
    row = lax.broadcasted_iota(jnp.int32, (512, 256), 0)
    column = lax.broadcasted_iota(jnp.int32, (512, 256), 1)
    for part in range(2):
        chosen = jnp.where(row == column * 2 + part, 1.0, 0.0).astype(BF)
        behind[:, part * 256 : (part + 1) * 256] = dot(chosen, single).astype(BF)
    value = jnp.sum(spread * eigen[...], axis=1, keepdims=True)
    order = lax.broadcasted_iota(jnp.int32, (1, MW), 1).astype(F32)
    ratio = order * (order + 1.0) / (MW * (MW - 1.0))
    scale[...] = 1.0 / (1.0 + value * ratio)
    for s, copy in enumerate(copies):
        copy.wait()
        turned[s] = dot(move.astype(BF), held[s]).astype(BF)


def prepare(modes, back, eigen, legendre):
    vmem = pl.BlockSpec(memory_space=pltpu.VMEM)
    return pl.pallas_call(
        prepare_kernel,
        out_shape=[
            jax.ShapeDtypeStruct((256, 256), BF),
            jax.ShapeDtypeStruct((512, 512), BF),
            jax.ShapeDtypeStruct((256, MW), F32),
            jax.ShapeDtypeStruct((5, NLAT, MW), BF),
        ],
        in_specs=[vmem] * 3 + [pl.BlockSpec(memory_space=pltpu.HBM)],
        out_specs=[vmem] * 4,
        scratch_shapes=[pltpu.VMEM((5, NLAT, MW), BF), pltpu.SemaphoreType.DMA((5,))],
        name="prepare",
        **params(16, flops=2 << 30, read=8 << 20),
    )(modes, back, eigen, legendre)


def receive_kernel(
    waves, moved, legendre, ahead, behind, scale, out, spread, latitude, projected, made, tables, sems, sems_out
):
    copies = [pltpu.make_async_copy(legendre.at[s], tables.at[s], sems.at[s]) for s in range(5)]
    for copy in copies:
        copy.start()
    for j in range(4):
        for lanes in range(2):
            mixed = jnp.concatenate(
                [
                    moved[lev * 640 : (lev + 1) * 640, j * 32 : (j + 1) * 32]
                    for lev in range(lanes * 4, lanes * 4 + 4)
                ],
                1,
            )
            spread[j, lanes] = mixed.astype(F32)

    def gather(s):
        for part in range(2):
            for j in range(4):
                for jq in range(2):
                    for lanes in range(2):
                        at = part * 256 + j * 64 + jq * 32
                        latitude[s, at : at + 32, lanes * BLK : (lanes + 1) * BLK] = spread[
                            j, lanes, pl.ds((2 * s + part) * 2 + jq, 32, stride=20), :
                        ].astype(BF)

    def project(s):
        projected[s] = dot_nt(ahead[...], latitude[s]).astype(BF)

    gather(0)
    project(0)
    first = (lax.axis_index("lev") * 32 + lax.axis_index("wave")) * 5
    order = lax.broadcasted_iota(jnp.int32, (1, MW), 1)
    sends = []
    def work(s, send):
        copies[s].wait()
        if s < 4:
            gather(s + 1)
        factor = jnp.where(order >= waves[first + s], scale[...], 0.0)
        scaled = [
            (dot(projected[s, :, part * 256 : (part + 1) * 256], tables[s]) * factor).astype(BF)
            for part in range(2)
        ]
        made.at[s].reshape(512, MW)[...] = dot(behind[...], jnp.concatenate(scaled, 0)).astype(BF)
        send.start()
        if s < 4:
            project(s + 1)

    for group in ((0, 1), (2, 3), (4,)):
        leaving = [
            pltpu.make_async_copy(made.at[s], out.at[pl.ds(s * 256, 256)], sems_out.at[s])
            for s in group
        ]

        @pl.when(waves[0] >= 0)
        def _(group=group, leaving=leaving):
            for s, send in zip(group, leaving):
                work(s, send)

        sends.extend(leaving)
    for send in sends:
        send.wait()


def receive(waves, moved, legendre, ahead, behind, scale):
    hbm = pl.BlockSpec(memory_space=pl.ANY)
    return pl.pallas_call(
        receive_kernel,
        out_shape=jax.ShapeDtypeStruct((5 * 256, 2, MW), BF),
        in_specs=[pl.BlockSpec(memory_space=pltpu.SMEM)]
        + [pl.BlockSpec(memory_space=pltpu.VMEM)]
        + [hbm]
        + [pl.BlockSpec(memory_space=pltpu.VMEM)] * 3,
        out_specs=hbm,
        scratch_shapes=[
            pltpu.VMEM((4, 2, 640, BLK), F32),
            pltpu.VMEM((5, 512, 256), BF),
            pltpu.VMEM((5, 256, 512), BF),
            pltpu.VMEM((5, 256, 2, MW), BF),
            pltpu.VMEM((5, NLAT, MW), BF),
            pltpu.SemaphoreType.DMA((5,)),
            pltpu.SemaphoreType.DMA((5,)),
        ],
        name="receive",
        **params(48, flops=6 << 30, read=14 << 20),
    )(waves, moved, legendre, ahead, behind, scale)


def shards(
    even, odd, grid, halo_values, halo_owner, halo_block, halo_count, wave_list, legendre, modes, back, eigen
):
    bands = lax.axis_size("wave")
    sent = pack(halo_owner, halo_block, halo_count, halo_values.reshape(SLOTS, 32, BLK))
    came = []
    for message, step in zip(sent, OFFSETS):
        route = [(i, (i + step) % bands) for i in range(bands)]
        came.append(lax.ppermute(message, "wave", route))
    grid, _ = lax.optimization_barrier((grid, sent))
    rows, even = ready(grid.reshape(32, 8, NLON), even)
    fourier = dft(came, wave_list.reshape(10, BLK), rows, even, odd)
    moved = lax.all_to_all(
        fourier.reshape(256, 5, 4, BLK), ("lev", "wave"), split_axis=0, concat_axis=0, tiled=True
    ).reshape(5120, BLK)
    legendre, _ = lax.optimization_barrier((legendre, fourier))
    ahead, behind, scale, turned = prepare(modes, back, eigen.reshape(1, LEV), legendre)
    result = receive(wave_list, moved, turned, ahead, behind, scale)
    return result.reshape(5, LEV, F, 2, MW)


def solution(mesh):
    placed = (
        P("lev", None, "wave", None),
        P("wave", None, "lev", None, None),
        P("wave", None),
        P("wave", None),
        P("wave"),
        P(),
        P(("lev", "wave"), None, None),
        P(),
        P(),
        P(),
    )
    mapped = jax.shard_map(
        shards,
        mesh=mesh,
        in_specs=(P(), P()) + placed,
        out_specs=P(("lev", "wave"), None, None, None, None),
        check_vma=False,
    )
    table = half_table()

    def whole(*args):
        return mapped(jnp.asarray(table[0]), jnp.asarray(table[1]), *args)

    return whole
```
